128 devices in a mesh: pb: 4 (over y_lo, core), kv: 32 (over x, y_hi, z).
Axes of the slice: x: 4, y: 4 (y_hi: 2, y_lo: 2; y = y_hi * 2 + y_lo), z: 4, core: 2. Of those that a mesh axis runs over, the one named last changes fastest.
Arguments:
- queries: bfloat16 [32768, 128], P(('pb', 'kv')), may hold values from -15 to 15
- query_tangent: bfloat16 [32768, 128], P(('pb', 'kv')), may hold values from -2 to 2
- keys: bfloat16 [32768, 128], P(('pb', 'kv')), may hold values from -8 to 8
- values: bfloat16 [32768, 128], P(('pb', 'kv')), may hold values from -6 to 6
- key_tangent: bfloat16 [32768, 128], P(('pb', 'kv')), may hold values from -2 to 2
- value_tangent: bfloat16 [32768, 128], P(('pb', 'kv')), may hold values from -6 to 6
- block_list: int32 [256, 32, 8], P('pb', 'kv'), may hold values from 0 to 255, as said below
- block_count: int32 [256, 32], P('pb', 'kv'), may hold values from 1 to 8, as said below
Outputs:
- attended: bfloat16 [32768, 128], P(('pb', 'kv'))
- attended_tangent: bfloat16 [32768, 128], P(('pb', 'kv'))
The draws below stay inside these ranges and needn't reach their ends.
Inputs may be any that keep to these rules, and one draw needn't show every extreme that they name: `block_list`: entries for one query block and slab j are distinct key blocks g whose index g // (256 // 128) leaves remainder j when divided by 32; entries past block_count are valid but unused. `block_count`: the value 8 is reached in every key slab.
All inputs are finite; a program needn't handle non-finite values.
Results may differ from the reference program's by a relative error of at most 0.01.
Values may be sent and summed in bfloat16 or wider, within the bound.
No kernel may reach another device: no remote copies, remote signals or barrier semaphores. Data moves between devices by JAX's collectives and lax.ppermute only.
A program may use at most 128 MiB of HBM per device.

```python
import math
import jax
import jax.numpy as jnp
from jax import lax

HD = 128
BLK = 128
LMAX = 8
TOK_DEV = 256
SEQ = 32768
QBLOCKS = 256
KSLABS = 32


def draw_queries(key, part):
    result = jnp.clip(2.5 * jax.random.normal(key, (SEQ, HD), jnp.float32), -15.0, 15.0)
    return result.astype(jnp.bfloat16)


def draw_keys(key, part):
    noise = jax.random.normal(jax.random.fold_in(key, 3), (SEQ, HD), jnp.float32)
    result = jnp.clip(noise, -6.0, 6.0)
    return result.astype(jnp.bfloat16)


def block_tables(key):
    base = jax.random.fold_in(key, 7)
    level_key, raw_key, force_key, order_key = jax.random.split(base, 4)
    slab_blocks = SEQ // (BLK * KSLABS)
    shard_blocks = TOK_DEV // BLK
    per_query_slab = QBLOCKS // (SEQ // (TOK_DEV * KSLABS))
    level = jax.random.randint(level_key, (SEQ // (TOK_DEV * KSLABS), KSLABS), 1, LMAX + 1)
    row_level = jnp.repeat(level, per_query_slab, axis=0)
    raw = jax.random.randint(raw_key, (QBLOCKS, KSLABS), 0, 1 << 20)
    counts = 1 + raw % row_level
    forced = jax.random.randint(force_key, (KSLABS,), 0, QBLOCKS)
    counts = jnp.where(jnp.arange(QBLOCKS)[:, None] == forced[None, :], LMAX, counts)
    ranks = jax.random.randint(order_key, (QBLOCKS, KSLABS, slab_blocks), 0, 1 << 20)
    ranks = ranks * slab_blocks + jnp.arange(slab_blocks)[None, None, :]
    picked = jnp.argsort(ranks, axis=-1, stable=True)[:, :, :LMAX]
    slab_index = jnp.arange(KSLABS)[None, :, None]
    global_block = (picked // shard_blocks * KSLABS + slab_index) * shard_blocks + picked % shard_blocks
    return (global_block.astype(jnp.int32), counts.astype(jnp.int32))


def draw_block_list(key, part):
    return block_tables(key)[0]


def draw_block_count(key, part):
    return block_tables(key)[1]


def steps_of(stream_key, dims, pieces, least, largest):
    def one(axis_at, parts):
        steps = jax.random.uniform(jax.random.fold_in(jax.random.fold_in(stream_key, 6), axis_at), (parts,), jnp.float32, least / len(pieces), largest / len(pieces))
        return jnp.repeat(jnp.exp(steps), dims[axis_at] // parts).reshape((-1,) + (1,) * (len(dims) - axis_at - 1))

    gain = one(*pieces[0])
    for cut in pieces[1:]:
        gain = gain * one(*cut)
    return gain


def bell_draw(stream_key, dims, deviation, limit, pieces=(), kind=jnp.bfloat16):
    values = jax.random.normal(stream_key, dims, jnp.float32) * deviation
    if len(pieces) > 0:
        values = steps_of(stream_key, dims, pieces, -0.22, 0.18) * values
    return jnp.clip(values, min=-limit, max=limit).astype(kind)


def setup_inputs(seed: int = 0) -> dict:
    streams_of = jax.random.split(jax.random.key(seed), 9)
    return {
        "queries": draw_queries(jax.random.fold_in(streams_of[8], 71), 0),
        "query_tangent": bell_draw(streams_of[1], (SEQ, HD), 0.3, 2.0, ((0, 128),)),
        "keys": draw_keys(jax.random.fold_in(streams_of[8], 71), 0),
        "values": bell_draw(streams_of[3], (SEQ, HD), 1.0, 6.0, ((0, 128),)),
        "key_tangent": bell_draw(streams_of[4], (SEQ, HD), 0.3, 2.0, ((0, 128),)),
        "value_tangent": bell_draw(streams_of[5], (SEQ, HD), 1.0, 6.0, ((0, 128),)),
        "block_list": draw_block_list(jax.random.fold_in(streams_of[8], 71), 0),
        "block_count": draw_block_count(jax.random.fold_in(streams_of[8], 71), 0),
    }


def reference(queries, query_tangent, keys, values, key_tangent, value_tangent, block_list, block_count):
    score_scale = 1.0 / math.sqrt(HD)
    key_blocks = keys.reshape(QBLOCKS, BLK, HD)
    value_blocks = values.reshape(QBLOCKS, BLK, HD)
    keyt_blocks = key_tangent.reshape(QBLOCKS, BLK, HD)
    valuet_blocks = value_tangent.reshape(QBLOCKS, BLK, HD)

    def one_block(items):
        query_block, tangent_block, picked, counts = items
        flat = picked.reshape(-1)
        key_rows = key_blocks[flat].reshape(-1, HD)
        value_rows = value_blocks[flat].reshape(-1, HD)
        keyt_rows = keyt_blocks[flat].reshape(-1, HD)
        valuet_rows = valuet_blocks[flat].reshape(-1, HD)
        active = jnp.repeat((jnp.arange(LMAX)[None, :] < counts[:, None]).reshape(-1), BLK)
        scores = jnp.dot(query_block, key_rows.T, preferred_element_type=jnp.float32) * score_scale
        score_tangent = (jnp.dot(tangent_block, key_rows.T, preferred_element_type=jnp.float32) + jnp.dot(query_block, keyt_rows.T, preferred_element_type=jnp.float32)) * score_scale
        peak = lax.optimization_barrier(jnp.max(jnp.where(active[None, :], scores, -jnp.inf), axis=1))
        weights = jnp.where(active[None, :], jnp.exp(scores - peak[:, None]), 0.0)
        total = lax.optimization_barrier(jnp.sum(weights, axis=1))
        slope = lax.optimization_barrier(jnp.sum(weights * score_tangent, axis=1))
        weights_b = weights.astype(jnp.bfloat16)
        scaled_b = (weights * score_tangent).astype(jnp.bfloat16)
        weighted = jnp.dot(weights_b, value_rows, preferred_element_type=jnp.float32)
        tangent_sum = jnp.dot(scaled_b, value_rows, preferred_element_type=jnp.float32) + jnp.dot(weights_b, valuet_rows, preferred_element_type=jnp.float32)
        output = weighted / total[:, None]
        output_tangent = tangent_sum / total[:, None] - (slope / total)[:, None] * output
        return (output.astype(jnp.bfloat16), output_tangent.astype(jnp.bfloat16))
    query_blocks = queries.reshape(QBLOCKS, BLK, HD)
    tangent_blocks = query_tangent.reshape(QBLOCKS, BLK, HD)
    attended, attended_tangent = lax.map(one_block, (query_blocks, tangent_blocks, block_list, block_count))
    return (attended.reshape(SEQ, HD), attended_tangent.reshape(SEQ, HD))
```

```python
import math

import jax
import jax.numpy as jnp
import numpy as np
from jax import lax
from jax.experimental import pallas as pl
from jax.experimental.pallas import tpu as pltpu
from jax.sharding import Mesh
from jax.sharding import PartitionSpec as P

BLK = 128
HD = 128
LMAX = 8
TOK = 256
NX, NZ = 4, 4
GROUP = 4
NKEY = 32
SCALE = 1.0 / math.sqrt(HD)
LOG2E = math.log2(math.e)
FLOOR = -1.0e30
STAT = 16
PART = 2 * BLK + STAT


def split3(x):
    hi = x.astype(jnp.bfloat16)
    rest = x - hi.astype(jnp.float32)
    mid = rest.astype(jnp.bfloat16)
    low = (rest - mid.astype(jnp.float32)).astype(jnp.bfloat16)
    return hi.astype(jnp.float32), mid.astype(jnp.float32), low.astype(jnp.float32)


def attend_kernel(me_ref, list_ref, *refs):
    q_refs, refs = refs[:8], refs[8:]
    k_refs, refs = refs[:16], refs[16:]
    out_refs, refs = refs[:8], refs[8:]
    kmat, vmat, x_ref, m_ref, sum_ref, slope_ref, acc_ref = refs
    my_yl, my_c, my_x, my_yh, my_z = (me_ref[i] for i in range(5))

    zero = jnp.zeros((BLK, HD), jnp.bfloat16)
    for shard, ref in enumerate(k_refs):
        for half in range(2):
            slot = shard * 2 + half
            rows = pl.ds(half * BLK, BLK)
            k = ref[pl.ds(half * BLK, BLK), :].T
            kt = ref[pl.ds(TOK + half * BLK, BLK), :].T
            v = ref[pl.ds(2 * TOK + half * BLK, BLK), :]
            vt = ref[pl.ds(3 * TOK + half * BLK, BLK), :]
            for mat, top, cross in ((kmat, k, kt), (vmat, v, vt)):
                mat[slot, :HD, :HD] = top
                mat[slot, :HD, HD:] = cross
                mat[slot, HD:, :HD] = zero
                mat[slot, HD:, HD:] = top

    for place in range(8):
        dyh, dz = place // 4, place % 4
        row0 = (my_yh ^ dyh) * 8 + ((my_z - dz + NZ) & 3) * 2
        q_ref, out_ref = q_refs[place], out_refs[place]
        bases, ends = [], []
        for sub in range(2):
            base = (row0 + sub) * 16
            stops, stop = [], jnp.int32(0)
            for sx in range(NX):
                stop = stop + list_ref[sx * 256 + base + LMAX]
                stops.append(stop)
            bases.append(base)
            ends.append(stops)
            x_ref[sub, :, :HD] = q_ref[pl.ds(sub * BLK, BLK), :]
            x_ref[sub, :, HD:] = q_ref[pl.ds(TOK + sub * BLK, BLK), :]
        m_ref[...] = jnp.full_like(m_ref, FLOOR)
        sum_ref[...] = jnp.zeros_like(sum_ref)
        slope_ref[...] = jnp.zeros_like(slope_ref)
        acc_ref[...] = jnp.zeros_like(acc_ref)

        def pick(sub, at):
            s0, s1, s2, s3 = ends[sub]
            penalty = jnp.where(at < s3, jnp.float32(0.0), jnp.float32(-FLOOR))
            at = jnp.minimum(at, s3 - 1)
            source = (
                (at >= s0).astype(jnp.int32) + (at >= s1).astype(jnp.int32) + (at >= s2).astype(jnp.int32)
            )
            first = jnp.where(at >= s2, s2, jnp.where(at >= s1, s1, jnp.where(at >= s0, s0, 0)))
            g = list_ref[source * 256 + bases[sub] + (at - first)]
            shard = g >> 1
            x, c, yl = (shard >> 3) & 3, (shard >> 5) & 1, (shard >> 6) & 1
            slot = ((((yl ^ my_yl) * 2 + (c ^ my_c)) * 4 + ((my_x - x + NX) & 3)) * 2) + (g & 1)
            return slot, penalty

        def step(n, carry):
            for sub in range(2):
                slots, dots = [], []
                for i in range(GROUP):
                    slot, penalty = pick(sub, n * GROUP + i)
                    slots.append((slot, penalty))
                    dots.append(
                        jnp.dot(x_ref[sub], kmat[slot], preferred_element_type=jnp.float32)
                    )
                top = dots[0][:, :HD]
                for d in dots[1:]:
                    top = jnp.maximum(top, d[:, :HD])
                top = jnp.max(top, axis=1, keepdims=True) * (SCALE * LOG2E)
                old = m_ref[sub]
                new = jnp.maximum(old, top)
                alpha = jnp.exp2(old - new)
                m_ref[sub] = new
                total = sum_ref[sub] * alpha
                slope = slope_ref[sub] * alpha
                part = None
                for d, (slot, penalty) in zip(dots, slots):
                    w = jnp.exp2(d[:, :HD] * (SCALE * LOG2E) - (new + penalty))
                    wt = w * (d[:, HD:] * SCALE)
                    total = total + w
                    slope = slope + wt
                    both = jnp.concatenate([w.astype(jnp.bfloat16), wt.astype(jnp.bfloat16)], axis=1)
                    term = jnp.dot(both, vmat[slot], preferred_element_type=jnp.float32)
                    part = term if part is None else part + term
                sum_ref[sub] = total
                slope_ref[sub] = slope
                acc_ref[sub, :, :HD] = acc_ref[sub, :, :HD] * alpha + part[:, :HD]
                acc_ref[sub, :, HD:] = acc_ref[sub, :, HD:] * alpha + part[:, HD:]
            return carry

        steps = (jnp.maximum(ends[0][3], ends[1][3]) + GROUP - 1) // GROUP
        lax.fori_loop(0, steps, step, 0)

        lane = lax.broadcasted_iota(jnp.int32, (BLK, HD), 1)
        for sub in range(2):
            total = jnp.sum(sum_ref[sub], axis=1, keepdims=True)
            inv = 1.0 / total
            slope = jnp.sum(slope_ref[sub], axis=1, keepdims=True) * inv
            o = acc_ref[sub, :, :HD] * inv
            t = acc_ref[sub, :, HD:] * inv - slope * o
            stats = jnp.zeros((BLK, HD), jnp.float32)
            for which, value in enumerate((m_ref[sub], total, slope)):
                for order, term in enumerate(split3(value)):
                    stats = jnp.where(lane == 3 * which + order, term, stats)
            base = sub * PART
            out_ref[pl.ds(base, BLK), :] = o.astype(jnp.bfloat16)
            out_ref[pl.ds(base + BLK, BLK), :] = t.astype(jnp.bfloat16)
            out_ref[pl.ds(base + 2 * BLK, STAT), :] = stats.T[:STAT, :].astype(jnp.bfloat16)


def combine_kernel(*refs):
    part_refs, (o_ref, t_ref) = refs[:8], refs[8:]
    for sub in range(2):
        base = sub * PART
        peaks, totals, slopes = [], [], []
        for ref in part_refs:
            stats = ref[pl.ds(base + 2 * BLK, STAT), :].astype(jnp.float32)
            for which, kept in enumerate((peaks, totals, slopes)):
                at = 3 * which
                kept.append(stats[at:at + 1] + stats[at + 1:at + 2] + stats[at + 2:at + 3])
        peak = peaks[0]
        for p in peaks[1:]:
            peak = jnp.maximum(peak, p)
        shares = [l * jnp.exp2(p - peak) for l, p in zip(totals, peaks)]
        inv = 1.0 / sum(shares[1:], shares[0])
        shares = [a * inv for a in shares]
        slope = sum((a * s for a, s in zip(shares[1:], slopes[1:])), shares[0] * slopes[0])
        cross = [a * (s - slope) for a, s in zip(shares, slopes)]
        rows = shares + cross + [jnp.zeros((HD - 16, BLK), jnp.float32)]
        columns = jnp.concatenate(rows, axis=0).T
        o = jnp.zeros((BLK, HD), jnp.float32)
        t = jnp.zeros((BLK, HD), jnp.float32)
        for j, ref in enumerate(part_refs):
            oj = ref[pl.ds(base, BLK), :].astype(jnp.float32)
            tj = ref[pl.ds(base + BLK, BLK), :].astype(jnp.float32)
            a, b = columns[:, j:j + 1], columns[:, 8 + j:9 + j]
            o = o + a * oj
            t = t + a * tj + b * oj
        o_ref[pl.ds(sub * BLK, BLK), :] = o.astype(jnp.bfloat16)
        t_ref[pl.ds(sub * BLK, BLK), :] = t.astype(jnp.bfloat16)


def shift(size, k):
    return [(i, (i + k) % size) for i in range(size)]


def shards(q, qt, k, v, kt, vt, block_list, block_count):
    me = jnp.stack([lax.axis_index(a) for a in ("yl", "c", "x", "yh", "z")]).astype(jnp.int32)
    vmem = pl.BlockSpec(memory_space=pltpu.VMEM)
    smem = pl.BlockSpec(memory_space=pltpu.SMEM)

    own = jnp.concatenate([k, kt, v, vt], axis=0)
    flip = [(0, 1), (1, 0)]
    beside = lax.ppermute(own, "yl", flip)
    held = [own] + [lax.ppermute(own, "x", shift(NX, d)) for d in (1, 2, 3)]
    forth = [None] * 4
    forth[0] = beside
    forth[1] = lax.ppermute(beside, "x", shift(NX, 1))
    forth[3] = lax.ppermute(beside, "x", shift(NX, 3))
    forth[2] = lax.ppermute(held[2], "yl", flip)
    other = lambda a: lax.ppermute(a, "c", flip)
    keys = held + [other(a) for a in held] + forth + [other(a) for a in forth]

    asked = jnp.concatenate([q, qt], axis=0)
    routes = []
    for dyh in range(2):
        for dz in range(NZ):
            routes.append([
                (yh * NZ + z, (yh ^ dyh) * NZ + (z + dz) % NZ) for yh in range(2) for z in range(NZ)
            ])
    queries = [asked] + [lax.ppermute(asked, ("yh", "z"), r) for r in routes[1:]]

    table = jnp.concatenate([block_list[:, 0, :], block_count, jnp.zeros((64, 7), jnp.int32)], axis=1)
    lists = lax.all_to_all(table.reshape(NX, 256), "x", 0, 0, tiled=True).reshape(-1)

    parts = pl.pallas_call(
        attend_kernel,
        out_shape=[jax.ShapeDtypeStruct((2 * PART, HD), jnp.bfloat16)] * 8,
        in_specs=[smem, smem] + [vmem] * 24,
        out_specs=[vmem] * 8,
        scratch_shapes=[
            pltpu.VMEM((NKEY, 2 * HD, 2 * HD), jnp.bfloat16),
            pltpu.VMEM((NKEY, 2 * HD, 2 * HD), jnp.bfloat16),
            pltpu.VMEM((2, BLK, 2 * HD), jnp.bfloat16),
            pltpu.VMEM((2, BLK, HD), jnp.float32),
            pltpu.VMEM((2, BLK, HD), jnp.float32),
            pltpu.VMEM((2, BLK, HD), jnp.float32),
            pltpu.VMEM((2, BLK, 2 * HD), jnp.float32),
        ],
        compiler_params=pltpu.CompilerParams(vmem_limit_bytes=40 * 2**20),
        name="attend",
    )(me, lists, *queries, *keys)

    back = [parts[0]]
    for r, part in zip(routes[1:], parts[1:]):
        back.append(lax.ppermute(part, ("yh", "z"), [(b, a) for a, b in r]))
    return tuple(
        pl.pallas_call(
            combine_kernel,
            out_shape=[jax.ShapeDtypeStruct((TOK, HD), jnp.bfloat16)] * 2,
            in_specs=[vmem] * 8,
            out_specs=[vmem] * 2,
            compiler_params=pltpu.CompilerParams(vmem_limit_bytes=16 * 2**20),
            name="combine",
        )(*back)
    )


def solution(mesh):
    split = Mesh(np.asarray(mesh.devices).reshape(2, 2, NX, 2, NZ), ("yl", "c", "x", "yh", "z"))
    pb, kv = ("yl", "c"), ("x", "yh", "z")
    row = P(pb + kv, None)
    return jax.shard_map(
        shards,
        mesh=split,
        in_specs=(row,) * 6 + (P(pb, kv, None), P(pb, kv)),
        out_specs=(row, row),
        check_vma=False,
    )
```

```python
import math

import jax
import jax.numpy as jnp
import numpy as np
from jax import lax
from jax.experimental import pallas as pl
from jax.experimental.pallas import tpu as pltpu
from jax.sharding import Mesh
from jax.sharding import PartitionSpec as P

BLK = 128
HD = 128
LMAX = 8
TOK = 256
NX, NZ = 4, 4
GROUP = 4
SCALE = 1.0 / math.sqrt(HD)
LOG2E = math.log2(math.e)
FLOOR = -1.0e30
STAT = 16
PART = 2 * BLK + STAT


def split3(x):
    hi = x.astype(jnp.bfloat16).astype(jnp.float32)
    mid = (x - hi).astype(jnp.bfloat16).astype(jnp.float32)
    return [hi, mid, x - hi - mid]


def attend_kernel(me_ref, *refs):
    tables, refs = refs[:4], refs[4:]
    q_refs, refs = refs[:4], refs[4:]
    k_refs, refs = refs[:10], refs[10:]
    out_refs, refs = refs[:8], refs[8:]
    q_buf, k_buf, vt_buf, wq_ref, m_ref, sum_ref, slope_ref, acc_ref, q_sem, k_sem = refs
    my_yl, my_c, my_x, my_yh, my_z = (me_ref[i] for i in range(5))

    q_copies = [pltpu.make_async_copy(ref, q_buf.at[i], q_sem.at[i]) for i, ref in enumerate(q_refs)]
    for copy in q_copies:
        copy.start()
    places = []
    for dc in range(2):
        for dx, dyl, size in ((0, 0, 2), (1, 0, 2), (3, 0, 2), (2, 0, 1), (2, 1, 1)):
            places.append(((dx * 2 + dc) * 2 + dyl, size))
    k_copies = []
    for i, (ref, (at, size)) in enumerate(zip(k_refs, places)):
        rows = pl.ds(at * 4 * TOK, size * 4 * TOK)
        k_copies.append(pltpu.make_async_copy(ref, k_buf.at[rows, :], k_sem.at[i]))
        k_copies[-1].start()
    for copy, (at, size) in zip(k_copies, places):
        copy.wait()
        for shard in range(at, at + size):
            for half in range(2):
                for part in range(2):
                    rows = pl.ds(shard * 4 * TOK + (2 + part) * TOK + half * BLK, BLK)
                    vt_buf[shard * 2 + half, pl.ds(part * HD, HD), :] = k_buf[rows, :].T
    for copy in q_copies:
        copy.wait()
    for sub in range(2):
        wq_ref[sub, HD:, :HD] = jnp.zeros((HD, BLK), jnp.bfloat16)

    for place in range(8):
        dyh, dz = place // 4, place % 4
        row0 = my_x * 16 + (my_yh ^ dyh) * 8 + ((my_z - dz + NZ) & 3) * 2
        ends = []
        for sub in range(2):
            stops, stop = [], jnp.int32(0)
            for table in tables:
                stop = stop + table[row0 + sub, LMAX]
                stops.append(stop)
            ends.append(stops)
            at = dyh * 2 * TOK + sub * BLK
            qx = q_buf[dz, pl.ds(at, BLK), :].T
            wq_ref[sub, :HD, :HD] = qx
            wq_ref[sub, HD:, HD:] = qx
            wq_ref[sub, :HD, HD:] = q_buf[dz, pl.ds(at + TOK, BLK), :].T
        m_ref[...] = jnp.full_like(m_ref, FLOOR)
        sum_ref[...] = jnp.zeros_like(sum_ref)
        slope_ref[...] = jnp.zeros_like(slope_ref)
        acc_ref[...] = jnp.zeros_like(acc_ref)

        def pick(sub, at):
            stops = ends[sub]
            penalty = jnp.where(at < stops[-1], jnp.float32(0.0), jnp.float32(-FLOOR))
            at = jnp.minimum(at, stops[-1] - 1)
            row = row0 + sub
            g = tables[0][row, jnp.minimum(at, LMAX - 1)]
            for table, stop in zip(tables[1:], stops):
                g = jnp.where(at >= stop, table[row, jnp.clip(at - stop, 0, LMAX - 1)], g)
            shard = g >> 1
            x, c, yl = (shard >> 3) & 3, (shard >> 5) & 1, (shard >> 6) & 1
            shard = ((((my_x - x + NX) & 3) * 2 + (c ^ my_c)) * 2) + (yl ^ my_yl)
            return shard, g & 1, penalty

        def step(n, carry):
            for sub in range(2):
                picked = [pick(sub, n * GROUP + i) for i in range(GROUP)]
                keys = []
                for shard, half, _ in picked:
                    at = pl.multiple_of(shard * (4 * TOK) + half * BLK, BLK)
                    keys.append(
                        jnp.concatenate([k_buf[pl.ds(at, BLK), :], k_buf[pl.ds(at + TOK, BLK), :]], axis=1)
                    )
                dots = jnp.dot(
                    jnp.concatenate(keys, axis=0), wq_ref[sub], preferred_element_type=jnp.float32
                )
                s, st = dots[:, :BLK], dots[:, BLK:]
                top = jnp.max(s, axis=0, keepdims=True) * (SCALE * LOG2E)
                old = m_ref[sub, 0:1, :]
                new = jnp.maximum(old, top)
                alpha = jnp.exp2(old - new)
                total = sum_ref[sub, 0:1, :] * alpha
                slope = slope_ref[sub, 0:1, :] * alpha
                both = []
                for i, (_, _, penalty) in enumerate(picked):
                    rows = slice(i * BLK, (i + 1) * BLK)
                    w = jnp.exp2(s[rows] * (SCALE * LOG2E) - (new + penalty))
                    wt = w * st[rows]
                    total = total + jnp.sum(w, axis=0, keepdims=True)
                    slope = slope + jnp.sum(wt, axis=0, keepdims=True)
                    both.append(
                        jnp.concatenate([w.astype(jnp.bfloat16), wt.astype(jnp.bfloat16)], axis=1)
                    )
                values = jnp.concatenate([vt_buf[shard * 2 + half] for shard, half, _ in picked], axis=1)
                out = jnp.dot(values, jnp.concatenate(both, axis=0), preferred_element_type=jnp.float32)
                m_ref[sub, 0:1, :] = new
                sum_ref[sub, 0:1, :] = total
                slope_ref[sub, 0:1, :] = slope
                acc_ref[sub, :HD, :] = acc_ref[sub, :HD, :] * alpha + out[:HD, :BLK]
                acc_ref[sub, HD:, :] = (
                    acc_ref[sub, HD:, :] * alpha + out[:HD, BLK:] * SCALE + out[HD:, :BLK]
                )
            return carry

        steps = (jnp.maximum(ends[0][-1], ends[1][-1]) + GROUP - 1) // GROUP
        lax.fori_loop(0, steps, step, 0)

        out_ref = out_refs[place]
        for sub in range(2):
            total = sum_ref[sub, 0:1, :]
            inv = 1.0 / total
            slope = slope_ref[sub, 0:1, :] * (inv * SCALE)
            o = acc_ref[sub, :HD, :] * inv
            t = acc_ref[sub, HD:, :] * inv - slope * o
            rows = split3(m_ref[sub, 0:1, :]) + split3(total) + split3(slope)
            rows.append(jnp.zeros((STAT - 9, BLK), jnp.float32))
            base = sub * PART
            out_ref[pl.ds(base, HD), :] = o.astype(jnp.bfloat16)
            out_ref[pl.ds(base + HD, HD), :] = t.astype(jnp.bfloat16)
            out_ref[pl.ds(base + 2 * HD, STAT), :] = jnp.concatenate(rows, axis=0).astype(jnp.bfloat16)


def combine_kernel(*refs):
    part_refs, (o_ref, t_ref) = refs[:8], refs[8:]
    for sub in range(2):
        base = sub * PART
        peaks, totals, slopes = [], [], []
        for ref in part_refs:
            stats = ref[pl.ds(base + 2 * HD, STAT), :].astype(jnp.float32)
            for which, kept in enumerate((peaks, totals, slopes)):
                at = 3 * which
                kept.append(stats[at:at + 1] + stats[at + 1:at + 2] + stats[at + 2:at + 3])
        peak = peaks[0]
        for p in peaks[1:]:
            peak = jnp.maximum(peak, p)
        shares = [l * jnp.exp2(p - peak) for l, p in zip(totals, peaks)]
        inv = 1.0 / sum(shares[1:], shares[0])
        shares = [a * inv for a in shares]
        slope = sum((a * s for a, s in zip(shares[1:], slopes[1:])), shares[0] * slopes[0])
        o = jnp.zeros((HD, BLK), jnp.float32)
        t = jnp.zeros((HD, BLK), jnp.float32)
        for ref, a, s in zip(part_refs, shares, slopes):
            oj = ref[pl.ds(base, HD), :].astype(jnp.float32)
            tj = ref[pl.ds(base + HD, HD), :].astype(jnp.float32)
            o = o + a * oj
            t = t + a * tj + (a * (s - slope)) * oj
        o_ref[pl.ds(sub * BLK, BLK), :] = o.T.astype(jnp.bfloat16)
        t_ref[pl.ds(sub * BLK, BLK), :] = t.T.astype(jnp.bfloat16)


def shift(size, k):
    return [(i, (i + k) % size) for i in range(size)]


def attend(me, tables, queries, keys):
    smem = pl.BlockSpec(memory_space=pltpu.SMEM)
    vmem = pl.BlockSpec(memory_space=pltpu.VMEM)
    anywhere = pl.BlockSpec(memory_space=pl.ANY)
    return pl.pallas_call(
        attend_kernel,
        out_shape=[jax.ShapeDtypeStruct((2 * PART, BLK), jnp.bfloat16)] * 8,
        in_specs=[smem] * 5 + [anywhere] * 14,
        out_specs=[vmem] * 8,
        scratch_shapes=[
            pltpu.VMEM((4, 4 * TOK, HD), jnp.bfloat16),
            pltpu.VMEM((16 * 4 * TOK, HD), jnp.bfloat16),
            pltpu.VMEM((32, 2 * HD, BLK), jnp.bfloat16),
            pltpu.VMEM((2, 2 * HD, 2 * BLK), jnp.bfloat16),
            pltpu.VMEM((2, 8, BLK), jnp.float32),
            pltpu.VMEM((2, 8, BLK), jnp.float32),
            pltpu.VMEM((2, 8, BLK), jnp.float32),
            pltpu.VMEM((2, 2 * HD, BLK), jnp.float32),
            pltpu.SemaphoreType.DMA((4,)),
            pltpu.SemaphoreType.DMA((10,)),
        ],
        compiler_params=pltpu.CompilerParams(vmem_limit_bytes=40 * 2**20),
        name="attend",
    )(me, *tables, *queries, *keys)


def shards(q, qt, k, v, kt, vt, block_list, block_count):
    me = jnp.stack([lax.axis_index(a) for a in ("yl", "c", "x", "yh", "z")]).astype(jnp.int32)
    flip = [(0, 1), (1, 0)]
    shard = 4 * TOK

    own = jnp.concatenate([k, kt, v, vt], axis=0)
    pair = jnp.concatenate([own, lax.ppermute(own, "yl", flip)], axis=0)
    ahead = lax.ppermute(pair, "x", shift(NX, 1))
    behind = lax.ppermute(pair, "x", shift(NX, 3))
    far0 = lax.ppermute(ahead[:shard], "x", shift(NX, 1))
    far1 = lax.ppermute(behind[shard:], "x", shift(NX, 3))
    keys = [pair, ahead, behind, far0, far1]
    keys = keys + [lax.ppermute(a, "c", flip) for a in keys]

    asked = jnp.concatenate([q, qt], axis=0)
    asked = jnp.concatenate([asked, lax.ppermute(asked, "yh", flip)], axis=0)
    queries = [asked] + [lax.ppermute(asked, "z", shift(NZ, d)) for d in (1, 2, 3)]

    table = jnp.concatenate([block_list[:, 0, :], block_count], axis=1)
    tables = [table] + [lax.ppermute(table, "x", shift(NX, d)) for d in (1, 2, 3)]

    parts = attend(me, tables, queries, keys)

    back = [parts[0]]
    for place in range(1, 8):
        dyh, dz = place // 4, place % 4
        route = [
            ((yh ^ dyh) * NZ + (z + dz) % NZ, yh * NZ + z) for yh in range(2) for z in range(NZ)
        ]
        back.append(lax.ppermute(parts[place], ("yh", "z"), route))
    vmem = pl.BlockSpec(memory_space=pltpu.VMEM)
    return tuple(
        pl.pallas_call(
            combine_kernel,
            out_shape=[jax.ShapeDtypeStruct((TOK, HD), jnp.bfloat16)] * 2,
            in_specs=[vmem] * 8,
            out_specs=[vmem] * 2,
            compiler_params=pltpu.CompilerParams(vmem_limit_bytes=16 * 2**20),
            name="combine",
        )(*back)
    )


def solution(mesh):
    split = Mesh(np.asarray(mesh.devices).reshape(2, 2, NX, 2, NZ), ("yl", "c", "x", "yh", "z"))
    pb, kv = ("yl", "c"), ("x", "yh", "z")
    row = P(pb + kv, None)
    return jax.shard_map(
        shards,
        mesh=split,
        in_specs=(row,) * 6 + (P(pb, kv, None), P(pb, kv)),
        out_specs=(row, row),
        check_vma=False,
    )
```

```python
import functools
import math

import jax
import jax.numpy as jnp
import numpy as np
from jax import lax
from jax.experimental import pallas as pl
from jax.experimental.pallas import tpu as pltpu
from jax.sharding import Mesh
from jax.sharding import PartitionSpec as P

BLK = 128
HD = 128
LMAX = 8
TOK = 256
NX, NZ = 4, 4
GROUP = 4
SCALE = 1.0 / math.sqrt(HD)
LOG2E = math.log2(math.e)
FLOOR = -1.0e30
STAT = 16
PART = 2 * BLK + STAT
PIECES = ((1, 0, 2), (3, 0, 2), (2, 0, 1), (2, 1, 1))


def split3(x):
    hi = x.astype(jnp.bfloat16).astype(jnp.float32)
    mid = (x - hi).astype(jnp.bfloat16).astype(jnp.float32)
    return [hi, mid, x - hi - mid]


class Job:
    def __init__(self, name, slabs, places, pieces, fresh, final, keep, group, room):
        self.name, self.slabs, self.places, self.pieces = name, slabs, places, pieces
        self.fresh, self.final, self.keep, self.group, self.room = fresh, final, keep, group, room


def attend_kernel(job, me_ref, *refs):
    refs = list(refs)

    def take(n):
        out = refs[:n]
        del refs[:n]
        return out

    group, count = job.group, len(job.slabs)
    tables_in = take(count)
    if job.fresh:
        q_refs = take(4)
    else:
        wq_in, state_in = take(2)
    if job.pieces:
        k_refs = take(len(job.pieces))
    else:
        k_buf, vt_buf = take(2)
    if job.fresh:
        wq_out, state_out = take(2)
    else:
        out_refs = take(len(job.places))
    if job.keep:
        k_buf, vt_buf = take(2)
    tables, s_ref, top_ref, m_ref, sum_ref, slope_ref, acc_ref, t_sem = take(8)
    if job.fresh:
        q_buf, q_sem = take(2)
    if job.pieces:
        raw, k_sem = take(2)
        if not job.keep:
            k_buf, vt_buf = take(2)
    my_yl, my_c, my_x, my_yh, my_z = (me_ref[i] for i in range(5))
    first_row = pl.multiple_of(my_x * 16, 16)

    t_copies = [
        pltpu.make_async_copy(ref.at[pl.ds(first_row, 16), :], tables.at[i], t_sem.at[i])
        for i, ref in enumerate(tables_in)
    ]
    for copy in t_copies:
        copy.start()
    if job.fresh:
        q_copies = [pltpu.make_async_copy(ref, q_buf.at[i], q_sem.at[i]) for i, ref in enumerate(q_refs)]
        for copy in q_copies:
            copy.start()
    if job.pieces:
        k_copies = []
        for i, (ref, (at, size)) in enumerate(zip(k_refs, job.pieces)):
            rows = pl.ds(at * 4 * TOK, size * 4 * TOK)
            k_copies.append(pltpu.make_async_copy(ref, raw.at[rows, :], k_sem.at[i]))
            k_copies[-1].start()
        for copy, (at, size) in zip(k_copies, job.pieces):
            copy.wait()
            for shard in range(at, at + size):
                for half in range(2):
                    slot = shard * 2 + half
                    for part in range(2):
                        rows = pl.ds(shard * 4 * TOK + part * TOK + half * BLK, BLK)
                        k_buf[pl.ds(slot * BLK, BLK), pl.ds(part * HD, HD)] = raw[rows, :]
                        rows = pl.ds(shard * 4 * TOK + (2 + part) * TOK + half * BLK, BLK)
                        vt_buf[slot, pl.ds(part * HD, HD), :] = raw[rows, :].T
    if job.fresh:
        for copy in q_copies:
            copy.wait()
    for copy in t_copies:
        copy.wait()
    base_dx = min(job.slabs)

    for nth, place in enumerate(job.places):
        dyh, dz = place // 4, place % 4
        row0 = (my_yh ^ dyh) * 8 + ((my_z - dz + NZ) & 3) * 2
        ends = []
        for sub in range(2):
            stops, stop = [], jnp.int32(0)
            for i in range(count):
                stop = stop + tables[i, row0 + sub, LMAX]
                stops.append(stop)
            ends.append(stops)
            if job.fresh:
                at = dyh * 2 * TOK + sub * BLK
                qx = q_buf[dz, pl.ds(at, BLK), :].T
                wq_out[place * 2 + sub, HD:, :HD] = jnp.zeros((HD, BLK), jnp.bfloat16)
                wq_out[place * 2 + sub, :HD, :HD] = qx
                wq_out[place * 2 + sub, HD:, HD:] = qx
                wq_out[place * 2 + sub, :HD, HD:] = q_buf[dz, pl.ds(at + TOK, BLK), :].T
        wq = wq_out if job.fresh else wq_in
        if job.fresh:
            m_ref[...] = jnp.full_like(m_ref, FLOOR)
            sum_ref[...] = jnp.zeros_like(sum_ref)
            slope_ref[...] = jnp.zeros_like(slope_ref)
            acc_ref[...] = jnp.zeros_like(acc_ref)
        else:
            for sub in range(2):
                m_ref[sub] = state_in[place * 2 + sub, 0:8, :]
                sum_ref[sub] = state_in[place * 2 + sub, 8:16, :]
                slope_ref[sub] = state_in[place * 2 + sub, 16:24, :]
                acc_ref[sub] = state_in[place * 2 + sub, 24:280, :]

        def pick(sub, at, ends=ends, row0=row0):
            stops = ends[sub]
            penalty = jnp.where(at < stops[-1], jnp.float32(0.0), jnp.float32(-FLOOR))
            at = jnp.minimum(at, stops[-1] - 1)
            row = row0 + sub
            g = tables[0, row, jnp.minimum(at, LMAX - 1)]
            for i, stop in enumerate(stops[:-1]):
                g = jnp.where(at >= stop, tables[i + 1, row, jnp.clip(at - stop, 0, LMAX - 1)], g)
            shard = g >> 1
            x, c, yl = (shard >> 3) & 3, (shard >> 5) & 1, (shard >> 6) & 1
            dx = (my_x - x + NX) & 3
            slot = ((((dx - base_dx) * 2 + (c ^ my_c)) * 2) + (yl ^ my_yl)) * 2 + (g & 1)
            return slot, penalty

        def score(sub, n, pick=pick, place=place):
            keys = []
            for i in range(group):
                slot, _ = pick(sub, n * group + i)
                keys.append(k_buf[pl.ds(pl.multiple_of(slot * BLK, BLK), BLK), :])
            dots = jnp.dot(
                jnp.concatenate(keys, axis=0), wq[place * 2 + sub], preferred_element_type=jnp.float32
            )
            s_ref[sub] = dots
            top_ref[sub, 0:1, :] = jnp.max(dots[:, :BLK], axis=0, keepdims=True) * (SCALE * LOG2E)

        def absorb(sub, n, pick=pick):
            picked = [pick(sub, n * group + i) for i in range(group)]
            old = m_ref[sub, 0:1, :]
            new = jnp.maximum(old, top_ref[sub, 0:1, :])
            alpha = jnp.exp2(old - new)
            total = sum_ref[sub, 0:1, :] * alpha
            slope = slope_ref[sub, 0:1, :] * alpha
            both = []
            for i, (_, penalty) in enumerate(picked):
                rows = pl.ds(i * BLK, BLK)
                w = jnp.exp2(s_ref[sub, rows, :BLK] * (SCALE * LOG2E) - (new + penalty))
                wt = w * s_ref[sub, rows, BLK:]
                total = total + jnp.sum(w, axis=0, keepdims=True)
                slope = slope + jnp.sum(wt, axis=0, keepdims=True)
                both.append(
                    jnp.concatenate([w.astype(jnp.bfloat16), wt.astype(jnp.bfloat16)], axis=1)
                )
            values = jnp.concatenate([vt_buf[slot] for slot, _ in picked], axis=1)
            out = jnp.dot(values, jnp.concatenate(both, axis=0), preferred_element_type=jnp.float32)
            m_ref[sub, 0:1, :] = new
            sum_ref[sub, 0:1, :] = total
            slope_ref[sub, 0:1, :] = slope
            acc_ref[sub, :HD, :] = acc_ref[sub, :HD, :] * alpha + out[:HD, :BLK]
            acc_ref[sub, HD:, :] = (
                acc_ref[sub, HD:, :] * alpha + out[:HD, BLK:] * SCALE + out[HD:, :BLK]
            )

        def step(n, carry, absorb=absorb, score=score):
            absorb(0, n)
            absorb(1, n)
            score(0, n + 1)
            score(1, n + 1)
            return carry

        steps = (jnp.maximum(ends[0][-1], ends[1][-1]) + group - 1) // group
        score(0, 0)
        score(1, 0)
        lax.fori_loop(0, steps - 1, step, 0)
        absorb(0, steps - 1)
        absorb(1, steps - 1)

        for sub in range(2):
            if not job.final:
                state_out[place * 2 + sub, 0:8, :] = m_ref[sub]
                state_out[place * 2 + sub, 8:16, :] = sum_ref[sub]
                state_out[place * 2 + sub, 16:24, :] = slope_ref[sub]
                state_out[place * 2 + sub, 24:280, :] = acc_ref[sub]
                continue
            out_ref = out_refs[nth]
            total = sum_ref[sub, 0:1, :]
            inv = 1.0 / total
            slope = slope_ref[sub, 0:1, :] * (inv * SCALE)
            o = acc_ref[sub, :HD, :] * inv
            t = acc_ref[sub, HD:, :] * inv - slope * o
            rows = split3(m_ref[sub, 0:1, :]) + split3(total) + split3(slope)
            rows.append(jnp.zeros((STAT - 9, BLK), jnp.float32))
            base = sub * PART
            out_ref[pl.ds(base, HD), :] = o.astype(jnp.bfloat16)
            out_ref[pl.ds(base + HD, HD), :] = t.astype(jnp.bfloat16)
            out_ref[pl.ds(base + 2 * HD, STAT), :] = jnp.concatenate(rows, axis=0).astype(jnp.bfloat16)


def stats_of(ref, base):
    stats = ref[pl.ds(base + 2 * HD, STAT), :].astype(jnp.float32)
    return [stats[3 * i:3 * i + 1] + stats[3 * i + 1:3 * i + 2] + stats[3 * i + 2:3 * i + 3] for i in range(3)]


def weigh(peaks, totals, slopes):
    peak = peaks[0]
    for p in peaks[1:]:
        peak = jnp.maximum(peak, p)
    shares = [l * jnp.exp2(p - peak) for l, p in zip(totals, peaks)]
    total = sum(shares[1:], shares[0])
    inv = 1.0 / total
    shares = [a * inv for a in shares]
    slope = sum((a * s for a, s in zip(shares[1:], slopes[1:])), shares[0] * slopes[0])
    return peak, total, slope, shares


def gather_kernel(*refs):
    part_refs, (o_ref, t_ref, stat_ref) = refs[:-3], refs[-3:]
    for sub in range(2):
        base = sub * PART
        peaks, totals, slopes = zip(*(stats_of(ref, base) for ref in part_refs))
        peak, total, slope, shares = weigh(peaks, totals, slopes)
        o = jnp.zeros((HD, BLK), jnp.float32)
        t = jnp.zeros((HD, BLK), jnp.float32)
        for ref, a, s in zip(part_refs, shares, slopes):
            oj = ref[pl.ds(base, HD), :].astype(jnp.float32)
            tj = ref[pl.ds(base + HD, HD), :].astype(jnp.float32)
            o = o + a * oj
            t = t + a * tj + (a * (s - slope)) * oj
        o_ref[sub] = o
        t_ref[sub] = t
        stat_ref[sub] = jnp.concatenate([peak, total, slope, jnp.zeros((5, BLK), jnp.float32)], axis=0)


def combine_kernel(o_in, t_in, stat_in, *refs):
    part_refs, (o_ref, t_ref) = refs[:-2], refs[-2:]
    for sub in range(2):
        base = sub * PART
        peaks, totals, slopes = zip(*(stats_of(ref, base) for ref in part_refs))
        first = [stat_in[sub, i:i + 1, :] for i in range(3)]
        peaks, totals, slopes = (first[0],) + peaks, (first[1],) + totals, (first[2],) + slopes
        _, _, slope, shares = weigh(peaks, totals, slopes)
        o = shares[0] * o_in[sub]
        t = shares[0] * t_in[sub] + (shares[0] * (slopes[0] - slope)) * o_in[sub]
        for ref, a, s in zip(part_refs, shares[1:], slopes[1:]):
            oj = ref[pl.ds(base, HD), :].astype(jnp.float32)
            tj = ref[pl.ds(base + HD, HD), :].astype(jnp.float32)
            o = o + a * oj
            t = t + a * tj + (a * (s - slope)) * oj
        o_ref[pl.ds(sub * BLK, BLK), :] = o.T.astype(jnp.bfloat16)
        t_ref[pl.ds(sub * BLK, BLK), :] = t.T.astype(jnp.bfloat16)


def shift(size, k):
    return [(i, (i + k) % size) for i in range(size)]


def attend(job, me, tables, *arrays):
    smem = pl.BlockSpec(memory_space=pltpu.SMEM)
    vmem = pl.BlockSpec(memory_space=pltpu.VMEM)
    anywhere = pl.BlockSpec(memory_space=pl.ANY)
    count, n_shards, n_out = len(job.slabs), 4 * len(job.slabs), len(job.places)
    shape = jax.ShapeDtypeStruct
    k_shape, v_shape = (n_shards * 2 * BLK, 2 * HD), (n_shards * 2, 2 * HD, BLK)
    in_specs = [smem] + [anywhere] * count
    in_specs += [anywhere] * 4 if job.fresh else [vmem] * 2
    in_specs += [anywhere] * len(job.pieces) if job.pieces else [vmem] * 2
    if job.fresh:
        outs = [shape((16, 2 * HD, 2 * BLK), jnp.bfloat16), shape((16, 24 + 2 * HD, BLK), jnp.float32)]
    else:
        outs = [shape((2 * PART, BLK), jnp.bfloat16)] * n_out
    if job.keep:
        outs = outs + [shape(k_shape, jnp.bfloat16), shape(v_shape, jnp.bfloat16)]
    scratch = [
        pltpu.SMEM((count, 16, 128), jnp.int32),
        pltpu.VMEM((2, job.group * BLK, 2 * BLK), jnp.float32),
        pltpu.VMEM((2, 8, BLK), jnp.float32),
        pltpu.VMEM((2, 8, BLK), jnp.float32),
        pltpu.VMEM((2, 8, BLK), jnp.float32),
        pltpu.VMEM((2, 8, BLK), jnp.float32),
        pltpu.VMEM((2, 2 * HD, BLK), jnp.float32),
        pltpu.SemaphoreType.DMA((count,)),
    ]
    if job.fresh:
        scratch += [pltpu.VMEM((4, 4 * TOK, HD), jnp.bfloat16), pltpu.SemaphoreType.DMA((4,))]
    if job.pieces:
        scratch += [
            pltpu.VMEM((n_shards * 4 * TOK, HD), jnp.bfloat16),
            pltpu.SemaphoreType.DMA((len(job.pieces),)),
        ]
        if not job.keep:
            scratch += [pltpu.VMEM(k_shape, jnp.bfloat16), pltpu.VMEM(v_shape, jnp.bfloat16)]
    pairs = 2 * n_out * count * 4
    return pl.pallas_call(
        functools.partial(attend_kernel, job),
        out_shape=outs,
        in_specs=in_specs,
        out_specs=[vmem] * len(outs),
        scratch_shapes=scratch,
        compiler_params=pltpu.CompilerParams(vmem_limit_bytes=job.room * 2**20),
        cost_estimate=pl.CostEstimate(
            flops=pairs * 60_000_000, bytes_accessed=4 * 2**20, transcendentals=pairs * BLK * BLK
        ),
        name=job.name,
    )(me, *tables, *arrays)


def shards(q, qt, k, v, kt, vt, block_list, block_count):
    me = jnp.stack([lax.axis_index(a) for a in ("yl", "c", "x", "yh", "z")]).astype(jnp.int32)
    flip = [(0, 1), (1, 0)]
    shard = 4 * TOK

    own = jnp.concatenate([k, kt, v, vt], axis=0)
    pair = jnp.concatenate([own, lax.ppermute(own, "yl", flip)], axis=0)
    table = jnp.concatenate([block_list[:, 0, :], block_count, jnp.zeros((64, 119), jnp.int32)], axis=1)
    tables = [table] + [lax.ppermute(table, "x", shift(NX, d)) for d in (1, 2, 3)]
    pair, *tables = lax.optimization_barrier((pair, *tables))
    ahead = lax.ppermute(pair, "x", shift(NX, 1))
    behind = lax.ppermute(pair, "x", shift(NX, 3))
    far0 = lax.ppermute(ahead[:shard], "x", shift(NX, 1))
    far1 = lax.ppermute(behind[shard:], "x", shift(NX, 3))
    mine = [pair, ahead, behind]
    theirs = [lax.ppermute(a, "c", flip) for a in mine]

    asked = jnp.concatenate([q, qt], axis=0)
    asked = jnp.concatenate([asked, lax.ppermute(asked, "yh", flip)], axis=0)
    queries = [asked] + [lax.ppermute(asked, "z", shift(NZ, d)) for d in (1, 2, 3)]

    near = Job("near", (0,), tuple(range(8)), [(0, 2), (2, 2)], True, False, False, 4, 12)
    pieces = [((dx - 1) * 4 + dc * 2 + dyl, n) for dc in range(2) for dx, dyl, n in PIECES]
    away = Job("away", (1, 2, 3), (4, 5, 6, 7), pieces, False, True, True, GROUP, 20)
    home = Job("home", (1, 2, 3), (0, 1, 2, 3), [], False, True, False, GROUP, 12)
    wq, state = attend(near, me, tables[:1], *queries, mine[0], theirs[0])
    far0, far1, wq, state = lax.optimization_barrier((far0, far1, wq, state))
    far = [far0, far1]
    mine = mine[1:] + far
    theirs = theirs[1:] + [lax.ppermute(a, "c", flip) for a in far]
    *outer, k_buf, vt_buf = attend(away, me, tables[1:], wq, state, *mine, *theirs)
    inner = attend(home, me, tables[1:], wq, state, k_buf, vt_buf)
    parts = list(inner) + list(outer)

    back = [parts[0]]
    for place in range(1, 8):
        dyh, dz = place // 4, place % 4
        route = [
            ((yh ^ dyh) * NZ + (z + dz) % NZ, yh * NZ + z) for yh in range(2) for z in range(NZ)
        ]
        back.append(lax.ppermute(parts[place], ("yh", "z"), route))
    vmem = pl.BlockSpec(memory_space=pltpu.VMEM)
    some = pl.pallas_call(
        gather_kernel,
        out_shape=[jax.ShapeDtypeStruct((2, n, BLK), jnp.float32) for n in (HD, HD, 8)],
        in_specs=[vmem] * 4,
        out_specs=[vmem] * 3,
        compiler_params=pltpu.CompilerParams(vmem_limit_bytes=8 * 2**20),
        name="gather",
    )(*back[4:])
    return tuple(
        pl.pallas_call(
            combine_kernel,
            out_shape=[jax.ShapeDtypeStruct((TOK, HD), jnp.bfloat16)] * 2,
            in_specs=[vmem] * 7,
            out_specs=[vmem] * 2,
            compiler_params=pltpu.CompilerParams(vmem_limit_bytes=8 * 2**20),
            name="combine",
        )(*some, *back[:4])
    )


def solution(mesh):
    split = Mesh(np.asarray(mesh.devices).reshape(2, 2, NX, 2, NZ), ("yl", "c", "x", "yh", "z"))
    pb, kv = ("yl", "c"), ("x", "yh", "z")
    row = P(pb + kv, None)
    return jax.shard_map(
        shards,
        mesh=split,
        in_specs=(row,) * 6 + (P(pb, kv, None), P(pb, kv)),
        out_specs=(row, row),
        check_vma=False,
    )
```

```python
import functools
import math

import jax
import jax.numpy as jnp
import numpy as np
from jax import lax
from jax.experimental import pallas as pl
from jax.experimental.pallas import tpu as pltpu
from jax.sharding import Mesh
from jax.sharding import PartitionSpec as P

BLK = 128
HD = 128
LMAX = 8
TOK = 256
NX, NZ = 4, 4
GROUP = 8
SCALE = 1.0 / math.sqrt(HD)
LOG2E = math.log2(math.e)
FLOOR = -1.0e30
STAT = 16
PART = 2 * BLK + STAT
PIECES = ((1, 0, 2), (3, 0, 2), (2, 0, 1), (2, 1, 1))


def split3(x):
    hi = x.astype(jnp.bfloat16).astype(jnp.float32)
    mid = (x - hi).astype(jnp.bfloat16).astype(jnp.float32)
    return [hi, mid, x - hi - mid]


class Job:
    def __init__(self, name, slabs, places, pieces, fresh, final, keep, group, room):
        self.name, self.slabs, self.places, self.pieces = name, slabs, places, pieces
        self.fresh, self.final, self.keep, self.group, self.room = fresh, final, keep, group, room


def attend_kernel(job, me_ref, *refs):
    refs = list(refs)

    def take(n):
        out = refs[:n]
        del refs[:n]
        return out

    group, count = job.group, len(job.slabs)
    tables_in = take(count)
    if job.fresh:
        q_refs = take(4)
    else:
        wq_in, state_in = take(2)
    if job.pieces:
        k_refs = take(len(job.pieces))
    else:
        k_buf, vt_buf = take(2)
    if job.fresh:
        wq_out, state_out = take(2)
    else:
        out_refs = take(len(job.places) // 2)
    if job.keep:
        k_buf, vt_buf = take(2)
    tables, s_ref, top_ref, m_ref, sum_ref, slope_ref, acc_ref, t_sem = take(8)
    if job.pieces and not job.keep:
        k_buf, vt_buf = take(2)
    my_yl, my_c, my_x, my_yh, my_z = (me_ref[i] for i in range(5))
    first_row = pl.multiple_of(my_x * 16, 16)

    t_copies = [
        pltpu.make_async_copy(ref.at[pl.ds(first_row, 16), :], tables.at[i], t_sem.at[i])
        for i, ref in enumerate(tables_in)
    ]
    for copy in t_copies:
        copy.start()
    if job.pieces:
        for ref, (at, size) in zip(k_refs, job.pieces):
            for shard in range(size):
                for half in range(2):
                    slot = (at + shard) * 2 + half
                    for part in range(2):
                        rows = pl.ds(shard * 4 * TOK + part * TOK + half * BLK, BLK)
                        k_buf[pl.ds(slot * BLK, BLK), pl.ds(part * HD, HD)] = ref[rows, :]
                        rows = pl.ds(shard * 4 * TOK + (2 + part) * TOK + half * BLK, BLK)
                        vt_buf[slot, pl.ds(part * HD, HD), :] = ref[rows, :].T
    for copy in t_copies:
        copy.wait()
    base_dx = min(job.slabs)

    wq = wq_out if job.fresh else wq_in

    def prepare(nth):
        place, side = job.places[nth], nth % 2
        dyh, dz = place // 4, place % 4
        row0 = (my_yh ^ dyh) * 8 + ((my_z - dz + NZ) & 3) * 2
        ends = []
        for sub in range(2):
            stops, stop = [], jnp.int32(0)
            for i in range(count):
                stop = stop + tables[i, row0 + sub, LMAX]
                stops.append(stop)
            ends.append(stops)
            if job.fresh:
                at = dyh * 2 * TOK + sub * BLK
                qx = q_refs[dz][pl.ds(at, BLK), :].T
                wq_out[place * 2 + sub, HD:, :HD] = jnp.zeros((HD, BLK), jnp.bfloat16)
                wq_out[place * 2 + sub, :HD, :HD] = qx
                wq_out[place * 2 + sub, HD:, HD:] = qx
                wq_out[place * 2 + sub, :HD, HD:] = q_refs[dz][pl.ds(at + TOK, BLK), :].T

        def pick(sub, at):
            stops = ends[sub]
            penalty = jnp.where(at < stops[-1], jnp.float32(0.0), jnp.float32(-FLOOR))
            at = jnp.minimum(at, stops[-1] - 1)
            row = row0 + sub
            g = tables[0, row, jnp.minimum(at, LMAX - 1)]
            for i, stop in enumerate(stops[:-1]):
                g = jnp.where(at >= stop, tables[i + 1, row, jnp.clip(at - stop, 0, LMAX - 1)], g)
            shard = g >> 1
            x, c, yl = (shard >> 3) & 3, (shard >> 5) & 1, (shard >> 6) & 1
            dx = (my_x - x + NX) & 3
            slot = ((((dx - base_dx) * 2 + (c ^ my_c)) * 2) + (yl ^ my_yl)) * 2 + (g & 1)
            return slot, penalty

        def score(sub, n):
            keys = []
            for i in range(group):
                slot, _ = pick(sub, n * group + i)
                keys.append(k_buf[pl.ds(pl.multiple_of(slot * BLK, BLK), BLK), :])
            dots = jnp.dot(
                jnp.concatenate(keys, axis=0), wq[place * 2 + sub], preferred_element_type=jnp.float32
            )
            s_ref[side, sub] = dots
            top_ref[side, sub, 0:1, :] = jnp.max(dots[:, :BLK], axis=0, keepdims=True) * (SCALE * LOG2E)

        def absorb(sub, n):
            picked = [pick(sub, n * group + i) for i in range(group)]
            old = m_ref[side, sub, 0:1, :]
            new = jnp.maximum(old, top_ref[side, sub, 0:1, :])
            alpha = jnp.exp2(old - new)
            total = sum_ref[side, sub, 0:1, :] * alpha
            slope = slope_ref[side, sub, 0:1, :] * alpha
            both = []
            for i, (_, penalty) in enumerate(picked):
                rows = pl.ds(i * BLK, BLK)
                w = jnp.exp2(s_ref[side, sub, rows, :BLK] * (SCALE * LOG2E) - (new + penalty))
                wt = w * s_ref[side, sub, rows, BLK:]
                total = total + jnp.sum(w, axis=0, keepdims=True)
                slope = slope + jnp.sum(wt, axis=0, keepdims=True)
                both.append(
                    jnp.concatenate([w.astype(jnp.bfloat16), wt.astype(jnp.bfloat16)], axis=1)
                )
            values = jnp.concatenate([vt_buf[slot] for slot, _ in picked], axis=1)
            out = jnp.dot(values, jnp.concatenate(both, axis=0), preferred_element_type=jnp.float32)
            m_ref[side, sub, 0:1, :] = new
            sum_ref[side, sub, 0:1, :] = total
            slope_ref[side, sub, 0:1, :] = slope
            acc_ref[side, sub, :HD, :] = acc_ref[side, sub, :HD, :] * alpha + out[:HD, :BLK]
            acc_ref[side, sub, HD:, :] = (
                acc_ref[side, sub, HD:, :] * alpha + out[:HD, BLK:] * SCALE + out[HD:, :BLK]
            )

        if group >= LMAX * count:
            steps = None
        else:
            steps = (jnp.maximum(ends[0][-1], ends[1][-1]) + group - 1) // group
        for sub in range(2):
            if job.fresh:
                m_ref[side, sub] = jnp.full((8, BLK), FLOOR, jnp.float32)
                sum_ref[side, sub] = jnp.zeros((8, BLK), jnp.float32)
                slope_ref[side, sub] = jnp.zeros((8, BLK), jnp.float32)
                acc_ref[side, sub] = jnp.zeros((2 * HD, BLK), jnp.float32)
            else:
                m_ref[side, sub] = state_in[place * 2 + sub, 0:8, :]
                sum_ref[side, sub] = state_in[place * 2 + sub, 8:16, :]
                slope_ref[side, sub] = state_in[place * 2 + sub, 16:24, :]
                acc_ref[side, sub] = state_in[place * 2 + sub, 24:280, :]
        score(0, 0)
        score(1, 0)
        return score, absorb, steps

    def finish(nth):
        place, side = job.places[nth], nth % 2
        for sub in range(2):
            if not job.final:
                state_out[place * 2 + sub, 0:8, :] = m_ref[side, sub]
                state_out[place * 2 + sub, 8:16, :] = sum_ref[side, sub]
                state_out[place * 2 + sub, 16:24, :] = slope_ref[side, sub]
                state_out[place * 2 + sub, 24:280, :] = acc_ref[side, sub]
                continue
            out_ref = out_refs[nth // 2]
            total = sum_ref[side, sub, 0:1, :]
            inv = 1.0 / total
            slope = slope_ref[side, sub, 0:1, :] * (inv * SCALE)
            o = acc_ref[side, sub, :HD, :] * inv
            t = acc_ref[side, sub, HD:, :] * inv - slope * o
            put(out_ref, (place // 4 * 2 + sub) * PART, o, t, m_ref[side, sub, 0:1, :], total, slope)

    ready = prepare(0)
    for nth in range(len(job.places)):
        score, absorb, steps = ready
        last = 0
        if steps is not None:
            last = steps - 1

            def step(n, carry, absorb=absorb, score=score):
                absorb(0, n)
                absorb(1, n)
                score(0, n + 1)
                score(1, n + 1)
                return carry

            lax.fori_loop(0, last, step, 0)
        if nth + 1 < len(job.places):
            ready = prepare(nth + 1)
        absorb(0, last)
        absorb(1, last)
        finish(nth)


def stats_of(ref, base):
    stats = ref[pl.ds(base + 2 * HD, STAT), :].astype(jnp.float32)
    return [stats[3 * i:3 * i + 1] + stats[3 * i + 1:3 * i + 2] + stats[3 * i + 2:3 * i + 3] for i in range(3)]


def weigh(peaks, totals, slopes):
    peak = peaks[0]
    for p in peaks[1:]:
        peak = jnp.maximum(peak, p)
    shares = [l * jnp.exp2(p - peak) for l, p in zip(totals, peaks)]
    total = sum(shares[1:], shares[0])
    inv = 1.0 / total
    shares = [a * inv for a in shares]
    slope = sum((a * s for a, s in zip(shares[1:], slopes[1:])), shares[0] * slopes[0])
    return peak, total, slope, shares


def merge(part_refs, at, sub):
    base = at + sub * PART
    peaks, totals, slopes = zip(*(stats_of(ref, base) for ref in part_refs))
    peak, total, slope, shares = weigh(peaks, totals, slopes)
    o = jnp.zeros((HD, BLK), jnp.float32)
    t = jnp.zeros((HD, BLK), jnp.float32)
    for ref, a, s in zip(part_refs, shares, slopes):
        oj = ref[pl.ds(base, HD), :].astype(jnp.float32)
        tj = ref[pl.ds(base + HD, HD), :].astype(jnp.float32)
        o = o + a * oj
        t = t + a * tj + (a * (s - slope)) * oj
    return o, t, peak, total, slope


def put(out_ref, base, o, t, peak, total, slope):
    rows = split3(peak) + split3(total) + split3(slope)
    rows.append(jnp.zeros((STAT - 9, BLK), jnp.float32))
    out_ref[pl.ds(base, HD), :] = o.astype(jnp.bfloat16)
    out_ref[pl.ds(base + HD, HD), :] = t.astype(jnp.bfloat16)
    out_ref[pl.ds(base + 2 * HD, STAT), :] = jnp.concatenate(rows, axis=0).astype(jnp.bfloat16)


def beyond_kernel(*refs):
    for sub in range(2):
        put(refs[-1], sub * PART, *merge(refs[:-1], 2 * PART, sub))


def within_kernel(*refs):
    part_refs, (o_ref, t_ref, stat_ref) = refs[:-3], refs[-3:]
    for sub in range(2):
        o, t, peak, total, slope = merge(part_refs, 0, sub)
        o_ref[sub] = o
        t_ref[sub] = t
        stat_ref[sub] = jnp.concatenate([peak, total, slope, jnp.zeros((5, BLK), jnp.float32)], axis=0)


def combine_kernel(o_in, t_in, stat_in, part, o_ref, t_ref):
    for sub in range(2):
        base = sub * PART
        first = [stat_in[sub, i:i + 1, :] for i in range(3)]
        second = stats_of(part, base)
        _, _, slope, (a, b) = weigh(*([p, q] for p, q in zip(first, second)))
        oj = part[pl.ds(base, HD), :].astype(jnp.float32)
        tj = part[pl.ds(base + HD, HD), :].astype(jnp.float32)
        o = a * o_in[sub] + b * oj
        t = a * t_in[sub] + b * tj + (a * (first[2] - slope)) * o_in[sub] + (b * (second[2] - slope)) * oj
        o_ref[pl.ds(sub * BLK, BLK), :] = o.T.astype(jnp.bfloat16)
        t_ref[pl.ds(sub * BLK, BLK), :] = t.T.astype(jnp.bfloat16)


def shift(size, k):
    return [(i, (i + k) % size) for i in range(size)]


def attend(job, me, tables, *arrays):
    smem = pl.BlockSpec(memory_space=pltpu.SMEM)
    vmem = pl.BlockSpec(memory_space=pltpu.VMEM)
    anywhere = pl.BlockSpec(memory_space=pl.ANY)
    count, n_shards, n_out = len(job.slabs), 4 * len(job.slabs), len(job.places)
    shape = jax.ShapeDtypeStruct
    k_shape, v_shape = (n_shards * 2 * BLK, 2 * HD), (n_shards * 2, 2 * HD, BLK)
    in_specs = [smem] + [anywhere] * count
    in_specs += [vmem] * 4 if job.fresh else [vmem] * 2
    in_specs += [vmem] * len(job.pieces) if job.pieces else [vmem] * 2
    if job.fresh:
        outs = [shape((16, 2 * HD, 2 * BLK), jnp.bfloat16), shape((16, 24 + 2 * HD, BLK), jnp.float32)]
    else:
        outs = [shape((4 * PART, BLK), jnp.bfloat16)] * (n_out // 2)
    if job.keep:
        outs = outs + [shape(k_shape, jnp.bfloat16), shape(v_shape, jnp.bfloat16)]
    scratch = [
        pltpu.SMEM((count, 16, 128), jnp.int32),
        pltpu.VMEM((2, 2, job.group * BLK, 2 * BLK), jnp.float32),
        pltpu.VMEM((2, 2, 8, BLK), jnp.float32),
        pltpu.VMEM((2, 2, 8, BLK), jnp.float32),
        pltpu.VMEM((2, 2, 8, BLK), jnp.float32),
        pltpu.VMEM((2, 2, 8, BLK), jnp.float32),
        pltpu.VMEM((2, 2, 2 * HD, BLK), jnp.float32),
        pltpu.SemaphoreType.DMA((count,)),
    ]
    if job.pieces and not job.keep:
        scratch += [pltpu.VMEM(k_shape, jnp.bfloat16), pltpu.VMEM(v_shape, jnp.bfloat16)]
    pairs = 2 * n_out * count * 4
    return pl.pallas_call(
        functools.partial(attend_kernel, job),
        out_shape=outs,
        in_specs=in_specs,
        out_specs=[vmem] * len(outs),
        scratch_shapes=scratch,
        compiler_params=pltpu.CompilerParams(vmem_limit_bytes=job.room * 2**20),
        cost_estimate=pl.CostEstimate(
            flops=pairs * 60_000_000, bytes_accessed=4 * 2**20, transcendentals=pairs * BLK * BLK
        ),
        name=job.name,
    )(me, *tables, *arrays)


def shards(q, qt, k, v, kt, vt, block_list, block_count):
    me = jnp.stack([lax.axis_index(a) for a in ("yl", "c", "x", "yh", "z")]).astype(jnp.int32)
    flip = [(0, 1), (1, 0)]
    shard = 4 * TOK

    own = jnp.concatenate([k, kt, v, vt], axis=0)
    own, block_list, block_count = lax.optimization_barrier((own, block_list, block_count))
    beside = lax.ppermute(own, "yl", flip)
    asked = jnp.concatenate([q, qt], axis=0)
    partner = lax.ppermute(asked, "yh", flip)
    table = jnp.concatenate([block_list[:, 0, :], block_count, jnp.zeros((64, 119), jnp.int32)], axis=1)
    tables = [table] + [lax.ppermute(table, "x", shift(NX, d)) for d in (1, 2, 3)]
    pair = jnp.concatenate([own, beside], axis=0)
    asked = jnp.concatenate([asked, partner], axis=0)
    pair, asked, *tables = lax.optimization_barrier((pair, asked, *tables))
    ahead = lax.ppermute(pair, "x", shift(NX, 1))
    behind = lax.ppermute(pair, "x", shift(NX, 3))
    far0 = lax.ppermute(ahead[:shard], "x", shift(NX, 1))
    far1 = lax.ppermute(behind[shard:], "x", shift(NX, 3))
    mine = [pair, ahead, behind]
    theirs = [lax.ppermute(a, "c", flip) for a in mine]

    queries = [asked] + [lax.ppermute(asked, "z", shift(NZ, d)) for d in (1, 2, 3)]

    near = Job("near", (0,), tuple(range(8)), [(0, 2), (2, 2)], True, False, False, GROUP, 12)
    pieces = [((dx - 1) * 4 + dc * 2 + dyl, n) for dc in range(2) for dx, dyl, n in PIECES]
    away = Job("away", (1, 2, 3), (1, 5, 2, 6, 3, 7), pieces, False, True, True, GROUP, 16)
    home = Job("home", (1, 2, 3), (0, 4), [], False, True, False, GROUP, 12)
    wq, state = attend(near, me, tables[:1], *queries, mine[0], theirs[0])
    far0, far1, wq, state = lax.optimization_barrier((far0, far1, wq, state))
    far = [far0, far1]
    mine = mine[1:] + far
    theirs = theirs[1:] + [lax.ppermute(a, "c", flip) for a in far]
    *outer, k_buf, vt_buf = attend(away, me, tables[1:], wq, state, *mine, *theirs)
    inner = attend(home, me, tables[1:], wq, state, k_buf, vt_buf)
    back = list(inner)
    for dz, part in zip((1, 2, 3), outer):
        back.append(lax.ppermute(part, "z", shift(NZ, NZ - dz)))
    theirs = small("beyond", beyond_kernel, [((2 * PART, BLK), jnp.bfloat16)], *back)[0]
    theirs = lax.ppermute(theirs, "yh", flip)
    own = small("within", within_kernel, [((2, n, BLK), jnp.float32) for n in (HD, HD, 8)], *back)
    return tuple(small("combine", combine_kernel, [((TOK, HD), jnp.bfloat16)] * 2, *own, theirs))


def small(name, kernel, outs, *arrays):
    vmem = pl.BlockSpec(memory_space=pltpu.VMEM)
    return pl.pallas_call(
        kernel,
        out_shape=[jax.ShapeDtypeStruct(*out) for out in outs],
        in_specs=[vmem] * len(arrays),
        out_specs=[vmem] * len(outs),
        compiler_params=pltpu.CompilerParams(vmem_limit_bytes=8 * 2**20),
        name=name,
    )(*arrays)


def solution(mesh):
    split = Mesh(np.asarray(mesh.devices).reshape(2, 2, NX, 2, NZ), ("yl", "c", "x", "yh", "z"))
    pb, kv = ("yl", "c"), ("x", "yh", "z")
    row = P(pb + kv, None)
    return jax.shard_map(
        shards,
        mesh=split,
        in_specs=(row,) * 6 + (P(pb, kv, None), P(pb, kv)),
        out_specs=(row, row),
        check_vma=False,
    )
```

```python
import functools
import math

import jax
import jax.numpy as jnp
import numpy as np
from jax import lax
from jax.experimental import pallas as pl
from jax.experimental.pallas import tpu as pltpu
from jax.sharding import Mesh
from jax.sharding import PartitionSpec as P

BLK = 128
HD = 128
LMAX = 8
TOK = 256
NX, NZ = 4, 4
GROUP = 8
SCALE = 1.0 / math.sqrt(HD)
LOG2E = math.log2(math.e)
FLOOR = -1.0e30
STAT = 16
PART = 2 * BLK + STAT
PIECES = ((1, 0, 2), (3, 0, 2), (2, 0, 1), (2, 1, 1))


def split3(x):
    hi = x.astype(jnp.bfloat16).astype(jnp.float32)
    mid = (x - hi).astype(jnp.bfloat16).astype(jnp.float32)
    return [hi, mid, x - hi - mid]


class Job:
    def __init__(self, name, slabs, places, pieces, fresh, final, keep, group, room):
        self.name, self.slabs, self.places, self.pieces = name, slabs, places, pieces
        self.fresh, self.final, self.keep, self.group, self.room = fresh, final, keep, group, room


def attend_kernel(job, me_ref, *refs):
    refs = list(refs)

    def take(n):
        out = refs[:n]
        del refs[:n]
        return out

    group, count = job.group, len(job.slabs)
    tables_in = take(count)
    if job.fresh:
        q_refs = take(4)
    else:
        wq_in, state_in = take(2)
    if job.pieces:
        k_refs = take(len(job.pieces))
    else:
        k_buf, vt_buf = take(2)
    if job.fresh:
        wq_out, state_out = take(2)
    else:
        out_refs = take(len(job.places) // 2)
    if job.keep:
        k_buf, vt_buf = take(2)
    tables, s_ref, top_ref, m_ref, sum_ref, slope_ref, acc_ref, t_sem = take(8)
    if job.pieces and not job.keep:
        k_buf, vt_buf = take(2)
    my_yl, my_c, my_x, my_yh, my_z = (me_ref[i] for i in range(5))
    first_row = pl.multiple_of(my_x * 16, 16)

    t_copies = [
        pltpu.make_async_copy(ref.at[pl.ds(first_row, 16), :], tables.at[i], t_sem.at[i])
        for i, ref in enumerate(tables_in)
    ]
    for copy in t_copies:
        copy.start()
    if job.pieces:
        for ref, (at, size) in zip(k_refs, job.pieces):
            for shard in range(size):
                for half in range(2):
                    slot = (at + shard) * 2 + half
                    for part in range(2):
                        rows = pl.ds(shard * 4 * TOK + part * TOK + half * BLK, BLK)
                        k_buf[pl.ds(slot * BLK, BLK), pl.ds(part * HD, HD)] = ref[rows, :]
                        rows = pl.ds(shard * 4 * TOK + (2 + part) * TOK + half * BLK, BLK)
                        vt_buf[slot, pl.ds(part * HD, HD), :] = ref[rows, :].T
    for copy in t_copies:
        copy.wait()
    base_dx = min(job.slabs)

    wq = wq_out if job.fresh else wq_in

    def prepare(nth):
        place, side = job.places[nth], nth % 2
        dyh, dz = place // 4, place % 4
        row0 = (my_yh ^ dyh) * 8 + ((my_z - dz + NZ) & 3) * 2
        ends = []
        for sub in range(2):
            stops, stop = [], jnp.int32(0)
            for i in range(count):
                stop = stop + tables[i, row0 + sub, LMAX]
                stops.append(stop)
            ends.append(stops)
            if job.fresh:
                at = dyh * 2 * TOK + sub * BLK
                qx = q_refs[dz][pl.ds(at, BLK), :].T
                wq_out[place * 2 + sub, HD:, :HD] = jnp.zeros((HD, BLK), jnp.bfloat16)
                wq_out[place * 2 + sub, :HD, :HD] = qx
                wq_out[place * 2 + sub, HD:, HD:] = qx
                wq_out[place * 2 + sub, :HD, HD:] = q_refs[dz][pl.ds(at + TOK, BLK), :].T

        def pick(sub, at):
            stops = ends[sub]
            penalty = jnp.where(at < stops[-1], jnp.float32(0.0), jnp.float32(-FLOOR))
            at = jnp.minimum(at, stops[-1] - 1)
            row = row0 + sub
            g = tables[0, row, jnp.minimum(at, LMAX - 1)]
            for i, stop in enumerate(stops[:-1]):
                g = jnp.where(at >= stop, tables[i + 1, row, jnp.clip(at - stop, 0, LMAX - 1)], g)
            shard = g >> 1
            x, c, yl = (shard >> 3) & 3, (shard >> 5) & 1, (shard >> 6) & 1
            dx = (my_x - x + NX) & 3
            slot = ((((dx - base_dx) * 2 + (c ^ my_c)) * 2) + (yl ^ my_yl)) * 2 + (g & 1)
            return slot, penalty

        def score(sub, n):
            keys = []
            for i in range(group):
                slot, _ = pick(sub, n * group + i)
                keys.append(k_buf[pl.ds(pl.multiple_of(slot * BLK, BLK), BLK), :])
            dots = jnp.dot(
                jnp.concatenate(keys, axis=0), wq[place * 2 + sub], preferred_element_type=jnp.float32
            )
            s_ref[side, sub] = dots
            top_ref[side, sub, 0:1, :] = jnp.max(dots[:, :BLK], axis=0, keepdims=True) * (SCALE * LOG2E)

        def absorb(sub, n):
            picked = [pick(sub, n * group + i) for i in range(group)]
            old = m_ref[side, sub, 0:1, :]
            new = jnp.maximum(old, top_ref[side, sub, 0:1, :])
            alpha = jnp.exp2(old - new)
            total = sum_ref[side, sub, 0:1, :] * alpha
            slope = slope_ref[side, sub, 0:1, :] * alpha
            both = []
            for i, (_, penalty) in enumerate(picked):
                rows = pl.ds(i * BLK, BLK)
                w = jnp.exp2(s_ref[side, sub, rows, :BLK] * (SCALE * LOG2E) - (new + penalty))
                wt = w * s_ref[side, sub, rows, BLK:]
                total = total + jnp.sum(w, axis=0, keepdims=True)
                slope = slope + jnp.sum(wt, axis=0, keepdims=True)
                both.append(
                    jnp.concatenate([w.astype(jnp.bfloat16), wt.astype(jnp.bfloat16)], axis=1)
                )
            values = jnp.concatenate([vt_buf[slot] for slot, _ in picked], axis=1)
            out = jnp.dot(values, jnp.concatenate(both, axis=0), preferred_element_type=jnp.float32)
            m_ref[side, sub, 0:1, :] = new
            sum_ref[side, sub, 0:1, :] = total
            slope_ref[side, sub, 0:1, :] = slope
            acc_ref[side, sub, :HD, :] = acc_ref[side, sub, :HD, :] * alpha + out[:HD, :BLK]
            acc_ref[side, sub, HD:, :] = (
                acc_ref[side, sub, HD:, :] * alpha + out[:HD, BLK:] * SCALE + out[HD:, :BLK]
            )

        if group >= LMAX * count:
            steps = None
        else:
            steps = (jnp.maximum(ends[0][-1], ends[1][-1]) + group - 1) // group
        for sub in range(2):
            if job.fresh:
                m_ref[side, sub] = jnp.full((8, BLK), FLOOR, jnp.float32)
                sum_ref[side, sub] = jnp.zeros((8, BLK), jnp.float32)
                slope_ref[side, sub] = jnp.zeros((8, BLK), jnp.float32)
                acc_ref[side, sub] = jnp.zeros((2 * HD, BLK), jnp.float32)
            else:
                m_ref[side, sub] = state_in[place * 2 + sub, 0:8, :]
                sum_ref[side, sub] = state_in[place * 2 + sub, 8:16, :]
                slope_ref[side, sub] = state_in[place * 2 + sub, 16:24, :]
                acc_ref[side, sub] = state_in[place * 2 + sub, 24:280, :]
        score(0, 0)
        score(1, 0)
        return score, absorb, steps

    def finish(nth):
        place, side = job.places[nth], nth % 2
        for sub in range(2):
            if not job.final:
                state_out[place * 2 + sub, 0:8, :] = m_ref[side, sub]
                state_out[place * 2 + sub, 8:16, :] = sum_ref[side, sub]
                state_out[place * 2 + sub, 16:24, :] = slope_ref[side, sub]
                state_out[place * 2 + sub, 24:280, :] = acc_ref[side, sub]
                continue
            out_ref = out_refs[nth // 2]
            total = sum_ref[side, sub, 0:1, :]
            inv = 1.0 / total
            slope = slope_ref[side, sub, 0:1, :] * (inv * SCALE)
            o = acc_ref[side, sub, :HD, :] * inv
            t = acc_ref[side, sub, HD:, :] * inv - slope * o
            put(out_ref, (place // 4 * 2 + sub) * PART, o, t, m_ref[side, sub, 0:1, :], total, slope)

    ready = prepare(0)
    for nth in range(len(job.places)):
        score, absorb, steps = ready
        last = 0
        if steps is not None:
            last = steps - 1

            def step(n, carry, absorb=absorb, score=score):
                absorb(0, n)
                absorb(1, n)
                score(0, n + 1)
                score(1, n + 1)
                return carry

            lax.fori_loop(0, last, step, 0)
        if nth + 1 < len(job.places):
            ready = prepare(nth + 1)
        absorb(0, last)
        absorb(1, last)
        finish(nth)


def stats_of(ref, base):
    stats = ref[pl.ds(base + 2 * HD, STAT), :].astype(jnp.float32)
    return [stats[3 * i:3 * i + 1] + stats[3 * i + 1:3 * i + 2] + stats[3 * i + 2:3 * i + 3] for i in range(3)]


def weigh(peaks, totals, slopes):
    peak = peaks[0]
    for p in peaks[1:]:
        peak = jnp.maximum(peak, p)
    shares = [l * jnp.exp2(p - peak) for l, p in zip(totals, peaks)]
    total = sum(shares[1:], shares[0])
    inv = 1.0 / total
    shares = [a * inv for a in shares]
    slope = sum((a * s for a, s in zip(shares[1:], slopes[1:])), shares[0] * slopes[0])
    return peak, total, slope, shares


def merge(part_refs, at, sub):
    base = at + sub * PART
    peaks, totals, slopes = zip(*(stats_of(ref, base) for ref in part_refs))
    peak, total, slope, shares = weigh(peaks, totals, slopes)
    o = jnp.zeros((HD, BLK), jnp.float32)
    t = jnp.zeros((HD, BLK), jnp.float32)
    for ref, a, s in zip(part_refs, shares, slopes):
        oj = ref[pl.ds(base, HD), :].astype(jnp.float32)
        tj = ref[pl.ds(base + HD, HD), :].astype(jnp.float32)
        o = o + a * oj
        t = t + a * tj + (a * (s - slope)) * oj
    return o, t, peak, total, slope


def put(out_ref, base, o, t, peak, total, slope):
    rows = split3(peak) + split3(total) + split3(slope)
    rows.append(jnp.zeros((STAT - 9, BLK), jnp.float32))
    out_ref[pl.ds(base, HD), :] = o.astype(jnp.bfloat16)
    out_ref[pl.ds(base + HD, HD), :] = t.astype(jnp.bfloat16)
    out_ref[pl.ds(base + 2 * HD, STAT), :] = jnp.concatenate(rows, axis=0).astype(jnp.bfloat16)


def beyond_kernel(*refs):
    for sub in range(2):
        put(refs[-1], sub * PART, *merge(refs[:-1], 2 * PART, sub))


def within_kernel(*refs):
    part_refs, (o_ref, t_ref, stat_ref) = refs[:-3], refs[-3:]
    for sub in range(2):
        o, t, peak, total, slope = merge(part_refs, 0, sub)
        o_ref[sub] = o
        t_ref[sub] = t
        stat_ref[sub] = jnp.concatenate([peak, total, slope, jnp.zeros((5, BLK), jnp.float32)], axis=0)


def combine_kernel(o_in, t_in, stat_in, part, o_ref, t_ref):
    for sub in range(2):
        base = sub * PART
        first = [stat_in[sub, i:i + 1, :] for i in range(3)]
        second = stats_of(part, base)
        _, _, slope, (a, b) = weigh(*([p, q] for p, q in zip(first, second)))
        oj = part[pl.ds(base, HD), :].astype(jnp.float32)
        tj = part[pl.ds(base + HD, HD), :].astype(jnp.float32)
        o = a * o_in[sub] + b * oj
        t = a * t_in[sub] + b * tj + (a * (first[2] - slope)) * o_in[sub] + (b * (second[2] - slope)) * oj
        o_ref[pl.ds(sub * BLK, BLK), :] = o.T.astype(jnp.bfloat16)
        t_ref[pl.ds(sub * BLK, BLK), :] = t.T.astype(jnp.bfloat16)


def shift(size, k):
    return [(i, (i + k) % size) for i in range(size)]


def attend(job, me, tables, *arrays):
    smem = pl.BlockSpec(memory_space=pltpu.SMEM)
    vmem = pl.BlockSpec(memory_space=pltpu.VMEM)
    anywhere = pl.BlockSpec(memory_space=pl.ANY)
    count, n_shards, n_out = len(job.slabs), 4 * len(job.slabs), len(job.places)
    shape = jax.ShapeDtypeStruct
    k_shape, v_shape = (n_shards * 2 * BLK, 2 * HD), (n_shards * 2, 2 * HD, BLK)
    in_specs = [smem] + [anywhere] * count
    in_specs += [vmem] * 4 if job.fresh else [vmem] * 2
    in_specs += [vmem] * len(job.pieces) if job.pieces else [vmem] * 2
    if job.fresh:
        outs = [shape((16, 2 * HD, 2 * BLK), jnp.bfloat16), shape((16, 24 + 2 * HD, BLK), jnp.float32)]
    else:
        outs = [shape((4 * PART, BLK), jnp.bfloat16)] * (n_out // 2)
    if job.keep:
        outs = outs + [shape(k_shape, jnp.bfloat16), shape(v_shape, jnp.bfloat16)]
    scratch = [
        pltpu.SMEM((count, 16, 128), jnp.int32),
        pltpu.VMEM((2, 2, job.group * BLK, 2 * BLK), jnp.float32),
        pltpu.VMEM((2, 2, 8, BLK), jnp.float32),
        pltpu.VMEM((2, 2, 8, BLK), jnp.float32),
        pltpu.VMEM((2, 2, 8, BLK), jnp.float32),
        pltpu.VMEM((2, 2, 8, BLK), jnp.float32),
        pltpu.VMEM((2, 2, 2 * HD, BLK), jnp.float32),
        pltpu.SemaphoreType.DMA((count,)),
    ]
    if job.pieces and not job.keep:
        scratch += [pltpu.VMEM(k_shape, jnp.bfloat16), pltpu.VMEM(v_shape, jnp.bfloat16)]
    pairs = 2 * n_out * count * 4
    return pl.pallas_call(
        functools.partial(attend_kernel, job),
        out_shape=outs,
        in_specs=in_specs,
        out_specs=[vmem] * len(outs),
        scratch_shapes=scratch,
        compiler_params=pltpu.CompilerParams(vmem_limit_bytes=job.room * 2**20),
        cost_estimate=pl.CostEstimate(
            flops=pairs * 60_000_000, bytes_accessed=4 * 2**20, transcendentals=pairs * BLK * BLK
        ),
        name=job.name,
    )(me, *tables, *arrays)


def shards(q, qt, k, v, kt, vt, block_list, block_count):
    me = jnp.stack([lax.axis_index(a) for a in ("yl", "c", "x", "yh", "z")]).astype(jnp.int32)
    flip = [(0, 1), (1, 0)]
    shard = 4 * TOK

    own = jnp.concatenate([k, kt, v, vt], axis=0)
    own, block_list, block_count = lax.optimization_barrier((own, block_list, block_count))
    beside = lax.ppermute(own, "yl", flip)
    asked = jnp.concatenate([q, qt], axis=0)
    partner = lax.ppermute(asked, "yh", flip)
    table = jnp.concatenate([block_list[:, 0, :], block_count, jnp.zeros((64, 119), jnp.int32)], axis=1)
    tables = [table] + [lax.ppermute(table, "x", shift(NX, d)) for d in (1, 2, 3)]
    pair = jnp.concatenate([own, beside], axis=0)
    asked = jnp.concatenate([asked, partner], axis=0)
    pair, asked, *tables = lax.optimization_barrier((pair, asked, *tables))
    ahead = lax.ppermute(pair, "x", shift(NX, 1))
    behind = lax.ppermute(pair, "x", shift(NX, 3))
    far0 = lax.ppermute(ahead[:shard], "x", shift(NX, 1))
    far1 = lax.ppermute(behind[shard:], "x", shift(NX, 3))
    mine = [pair, ahead, behind]
    theirs = [lax.ppermute(a, "c", flip) for a in mine]

    queries = [asked] + [lax.ppermute(asked, "z", shift(NZ, d)) for d in (1, 2, 3)]

    near = Job("near", (0,), tuple(range(8)), [(0, 2), (2, 2)], True, False, False, GROUP, 12)
    pieces = [((dx - 1) * 4 + dc * 2 + dyl, n) for dc in range(2) for dx, dyl, n in PIECES]
    away = Job("away", (1, 2, 3), (2, 6, 1, 5, 3, 7), pieces, False, True, True, GROUP, 16)
    home = Job("home", (1, 2, 3), (0, 4), [], False, True, False, GROUP, 12)
    wq, state = attend(near, me, tables[:1], *queries, mine[0], theirs[0])
    far0, far1, wq, state = lax.optimization_barrier((far0, far1, wq, state))
    far = [far0, far1]
    mine = mine[1:] + far
    theirs = theirs[1:] + [lax.ppermute(a, "c", flip) for a in far]
    *outer, k_buf, vt_buf = attend(away, me, tables[1:], wq, state, *mine, *theirs)
    inner = attend(home, me, tables[1:], wq, state, k_buf, vt_buf)
    back = list(inner)
    for dz, part in zip((2, 1, 3), outer):
        back.append(lax.ppermute(part, "z", shift(NZ, NZ - dz)))
    theirs = small("beyond", beyond_kernel, [((2 * PART, BLK), jnp.bfloat16)], *back)[0]
    theirs = lax.ppermute(theirs, "yh", flip)
    own = small("within", within_kernel, [((2, n, BLK), jnp.float32) for n in (HD, HD, 8)], *back)
    return tuple(small("combine", combine_kernel, [((TOK, HD), jnp.bfloat16)] * 2, *own, theirs))


def small(name, kernel, outs, *arrays):
    vmem = pl.BlockSpec(memory_space=pltpu.VMEM)
    return pl.pallas_call(
        kernel,
        out_shape=[jax.ShapeDtypeStruct(*out) for out in outs],
        in_specs=[vmem] * len(arrays),
        out_specs=[vmem] * len(outs),
        compiler_params=pltpu.CompilerParams(vmem_limit_bytes=8 * 2**20),
        name=name,
    )(*arrays)


def solution(mesh):
    split = Mesh(np.asarray(mesh.devices).reshape(2, 2, NX, 2, NZ), ("yl", "c", "x", "yh", "z"))
    pb, kv = ("yl", "c"), ("x", "yh", "z")
    row = P(pb + kv, None)
    return jax.shard_map(
        shards,
        mesh=split,
        in_specs=(row,) * 6 + (P(pb, kv, None), P(pb, kv)),
        out_specs=(row, row),
        check_vma=False,
    )
```
